32 devices in a mesh: band: 16 (over z, y, x), strip: 2 (over core).
Axes of the slice: x: 2, y: 2, z: 4, core: 2. Of those that a mesh axis runs over, the one named last changes fastest.
Arguments:
- coeffs: bfloat16 [128, 128, 2048], P('strip', None, 'band'), may hold values from -4.1875 to 4.1875
- hamiltonian: bfloat16 [128, 5, 128, 128], P('strip'), may hold values from -0.15625 to 0.15625
- adjacency: int32 [128, 5], P('strip'), may hold values from 0 to 127, as said below
- occupation: float32 [2048], P('band'), may hold values from 0.1 to 2
Outputs:
- density: float32 [128, 128, 128], P(('strip', 'band'))
The draws below stay inside these ranges and needn't reach their ends.
Inputs may be any that keep to these rules, and one draw needn't show every extreme that they name: `adjacency`: row e lists element e itself and its four neighbours on the periodic 8 x 16 sheet of elements, numbered row * 16 + column, in an order drawn for each element.
All inputs are finite; a program needn't handle non-finite values.
Results may differ from the reference program's by a relative error of at most 0.019.
Values may be sent and summed in bfloat16 or wider, within the bound.
A program may use at most 128 MiB of HBM per device.

```python
import math
import jax
import jax.numpy as jnp
from jax import lax

NB = 128
EY = 16
EX = 8
ELEMS = 128
NBAND = 2048


def draw_adjacency(key, part):
    element = jnp.arange(ELEMS, dtype=jnp.int32)
    elem_row = element // EY
    elem_col = element % EY
    candidates = jnp.stack([element, (elem_row + 1) % EX * EY + elem_col, (elem_row - 1 + EX) % EX * EY + elem_col, elem_row * EY + (elem_col + 1) % EY, elem_row * EY + (elem_col - 1 + EY) % EY], axis=1)
    scores = jax.random.randint(key, (ELEMS, 5), 0, 1 << 20, dtype=jnp.int32) * 8 + jnp.arange(5, dtype=jnp.int32)
    ordering = jnp.argsort(scores, axis=1, stable=True)
    return jnp.take_along_axis(candidates, ordering, axis=1).astype(jnp.int32)


def shard_levels(own_key, extent, cuts, least, top_value):
    def one(axis_at, parts):
        heights = jax.random.uniform(jax.random.fold_in(jax.random.fold_in(own_key, 6), axis_at), (parts,), jnp.float32, least / len(cuts), top_value / len(cuts))
        return jnp.repeat(jnp.exp(heights), extent[axis_at] // parts).reshape((-1,) + (1,) * (len(extent) - axis_at - 1))

    factor_of = one(*cuts[0])
    for cut in cuts[1:]:
        factor_of = factor_of * one(*cut)
    return factor_of


def scatter_about(stream_key, shape, scale, most, shards=(), held_as=jnp.bfloat16):
    values = scale * jax.random.normal(stream_key, shape, jnp.float32)
    if shards:
        values = values * shard_levels(stream_key, shape, shards, -0.22, 0.18)
    return jnp.clip(values, -most, most).astype(held_as)


def setup_inputs(seed: int = 0) -> dict:
    splits = jax.random.split(jax.random.key(seed), 5)
    return {
        "coeffs": scatter_about(splits[0], (ELEMS, NB, NBAND), 0.7, 4.1875, ((0, 2), (2, 16))),
        "hamiltonian": scatter_about(splits[1], (ELEMS, 5, NB, NB), (10 * NB) ** -0.5, 0.15625, ((0, 2),)),
        "adjacency": draw_adjacency(jax.random.fold_in(splits[4], 71), 0),
        "occupation": jnp.clip(jnp.exp(math.log(2.0) - 2.9957323 * jax.random.uniform(splits[3], (NBAND,), jnp.float32) ** shard_levels(splits[3], (NBAND,), ((0, 16),), -0.2, 0.2)), 0.1, 2.0),
    }


def apply_operator(field_block, hamiltonian_wide, adjacency):
    total = jnp.zeros(field_block.shape, jnp.float32)
    for slot_index in range(5):
        neighbours = field_block[adjacency[:, slot_index]].astype(jnp.float32)
        total = total + jnp.einsum("eik,ekb->eib", hamiltonian_wide[:, slot_index], neighbours)
    return total


def reference(coeffs, hamiltonian, adjacency, occupation):
    hamiltonian_wide = hamiltonian.astype(jnp.float32)
    block_width = math.gcd(NBAND, 512)
    blocks = NBAND // block_width
    coeff_blocks = jnp.moveaxis(coeffs.reshape(ELEMS, NB, blocks, block_width), 2, 0)
    occ_blocks = occupation.reshape(blocks, block_width)

    def one_block(accumulated, inputs):
        coeff_block, occ_block = inputs
        degree_one = apply_operator(coeff_block, hamiltonian_wide, adjacency).astype(jnp.bfloat16)
        degree_two = (2.0 * apply_operator(degree_one, hamiltonian_wide, adjacency) - coeff_block.astype(jnp.float32)).astype(jnp.bfloat16)
        filtered = (2.0 * apply_operator(degree_two, hamiltonian_wide, adjacency) - degree_one.astype(jnp.float32)).astype(jnp.bfloat16)
        weighted = (filtered.astype(jnp.float32) * occ_block).astype(jnp.bfloat16)
        accumulated = accumulated + jnp.einsum("eib,ejb->eij", weighted.astype(jnp.float32), filtered.astype(jnp.float32))
        return accumulated, None

    summed, unused = lax.scan(one_block, jnp.zeros((ELEMS, NB, NB), jnp.float32), (coeff_blocks, occ_blocks))
    return summed / NBAND
```

```python
import functools
import jax
import jax.numpy as jnp
from jax import lax
from jax.experimental import pallas as pl
from jax.experimental.pallas import tpu as pltpu
from jax.sharding import PartitionSpec as P

EY = 16
PAD = 16
MIB = 1 << 20


def lanes(shape):
    return lax.broadcasted_iota(jnp.int32, shape, 1)


def rows(shape):
    return lax.broadcasted_iota(jnp.int32, shape, 0)


def pack_pair(first, second):
    half = first.shape[0] // 2
    left = lanes((half, 2 * half)) < half
    lane = jnp.where(left, lanes(left.shape), lanes(left.shape) - half)
    row = rows(left.shape)
    blocks_1 = jnp.where(left, first[:half], first[half:])
    blocks_2 = jnp.where(left, second[:half], second[half:])
    triangles = jnp.where(row >= lane, blocks_1, blocks_2)
    corners = jnp.where(left, second[half:], first[:half])
    diagonal = jnp.sum(jnp.where(row == lane, blocks_2, 0.0), axis=0, keepdims=True)
    return jnp.concatenate(
        [triangles, corners, jnp.broadcast_to(diagonal, (PAD, 2 * half))], axis=0
    )


def unpack_pair(packed):
    nb = packed.shape[1]
    half = nb // 2
    triangles, corners, diagonal = packed[:half], packed[half:nb], packed[nb:nb + 1]
    left = lanes((half, nb)) < half
    i, j = rows((nb, nb)), lanes((nb, nb))
    same = (i < half) == (j < half)
    wide_1 = jnp.concatenate([jnp.where(left, triangles, corners), triangles], axis=0)
    held_1 = (same & (i >= j)) | ((i < half) & (j >= half))
    first = jnp.where(held_1, wide_1, wide_1.T)
    wide_2 = jnp.concatenate([triangles, jnp.where(left, corners, triangles)], axis=0)
    held_2 = (same & (i < j)) | ((i >= half) & (j < half))
    second = jnp.where(held_2, wide_2, wide_2.T)
    second = jnp.where(i == j, jnp.broadcast_to(diagonal, (nb, nb)), second)
    return first, second


def kernel(
    strips, bands, total_bands,
    adj_ref, occ_ref, coeffs_hbm, ham_hbm, out_ref,
    ham, v0, v1, v2, packed, arrived, crossed, slots,
    ham_sem, v0_sem, halo_send, halo_recv, part_send, part_recv, cross_send, cross_recv,
):
    elems = coeffs_hbm.shape[0]
    row_count = elems // EY
    group = bands // row_count
    bits = group.bit_length() - 1
    owned = EY // group
    pairs = owned // 2
    strip = lax.axis_index("strip")
    band = lax.axis_index("band")
    my_row, mine = band // group, band % group
    above, below = (strip + strips - 1) % strips, (strip + 1) % strips

    def partner(bit):
        step = 1 << bit
        return band + step * (1 - 2 * ((band // step) % 2))

    own_copy = pltpu.make_async_copy(coeffs_hbm, v0.at[pl.ds(EY, elems)], v0_sem)
    own_copy.start()
    per_row = EY * 5
    ham_copies = [
        pltpu.make_async_copy(
            ham_hbm.at[pl.ds(r * per_row, per_row)], ham.at[pl.ds(r * per_row, per_row)], ham_sem.at[r]
        )
        for r in range(row_count)
    ]
    row_order = [1, 0] + [row_count - 1] + list(range(2, row_count - 1))
    for r in row_order:
        ham_copies[r].start()

    barrier = pltpu.get_barrier_semaphore()
    greeted = 0
    for target in [above] if strips == 2 else [above, below]:
        pl.semaphore_signal(barrier, inc=1, device_id={"strip": target})
        greeted += 1
    for bit in range(bits):
        pl.semaphore_signal(barrier, inc=1, device_id={"band": partner(bit)})
        greeted += 1
    for away in range(1, row_count):
        pl.semaphore_signal(
            barrier, inc=1, device_id={"band": ((my_row + away) % row_count) * group + mine}
        )
        greeted += 1
    pl.semaphore_wait(barrier, greeted)

    def halo(field, ref, source, shift):
        up = pltpu.make_async_remote_copy(
            source.at[pl.ds(shift, EY)], ref.at[pl.ds(EY + elems, EY)],
            halo_send.at[2 * field], halo_recv.at[2 * field], device_id={"strip": above},
        )
        down = pltpu.make_async_remote_copy(
            source.at[pl.ds(shift + elems - EY, EY)], ref.at[pl.ds(0, EY)],
            halo_send.at[2 * field + 1], halo_recv.at[2 * field + 1], device_id={"strip": below},
        )
        return up, down

    halos = [halo(0, v0, coeffs_hbm, 0), halo(1, v1, v1, EY), halo(2, v2, v2, EY)]
    for copy in halos[0]:
        copy.start()

    def product(blocks, fields):
        return jnp.dot(
            jnp.concatenate(blocks, axis=1), jnp.concatenate(fields, axis=0),
            preferred_element_type=jnp.float32,
        )

    sheet_rows = row_count * strips

    def first_element(r, c):
        e = r * EY + c
        places = []
        for j in range(5):
            a = adj_ref[e, j]
            rel = lax.rem(lax.div(a, EY) - strip * row_count + (1 + sheet_rows), sheet_rows)
            places.append(rel * EY + lax.rem(a, EY))
        here = e + EY
        wanted = [
            here, here - EY, here + EY,
            (r + 1) * EY + lax.rem(c + EY - 1, EY), (r + 1) * EY + lax.rem(c + 1, EY),
        ]
        for d in range(5):
            slot = jnp.int32(0)
            for j in range(1, 5):
                slot = slot + jnp.where(places[j] == wanted[d], jnp.int32(j), jnp.int32(0))
            slots[e * 5 + d] = slot
        out = product([ham[e * 5 + j] for j in range(5)], [v0[p] for p in places])
        v1[here] = out.astype(jnp.bfloat16)

    def later_product(ref, r, c):
        e = r * EY + c
        here = e + EY
        line = (r + 1) * EY
        fields = [
            ref[here], ref[here - EY], ref[here + EY],
            ref[line + lax.rem(c + EY - 1, EY)], ref[line + lax.rem(c + 1, EY)],
        ]
        return product([ham[e * 5 + slots[e * 5 + d]] for d in range(5)], fields)

    def second_element(r, c):
        here = r * EY + c + EY
        out = 2.0 * later_product(v1, r, c) - v0[here].astype(jnp.float32)
        v2[here] = out.astype(jnp.bfloat16)

    STEP = 4

    def one_row(element, r):
        def body(g, carry):
            for m in range(STEP):
                element(r, g * STEP + m)
            return carry

        lax.fori_loop(0, EY // STEP, body, 0)

    own_copy.wait()
    for copy in halos[0]:
        copy.wait_recv()
    for r in row_order:
        ham_copies[r].wait()
        one_row(first_element, r)
        if r == 0:
            halos[1][0].start()
        if r == row_count - 1:
            halos[1][1].start()
    for r in row_order:
        if r == 0:
            halos[1][1].wait_recv()
        if r == row_count - 1:
            halos[1][0].wait_recv()
        one_row(second_element, r)
        if r == 0:
            halos[2][0].start()
        if r == row_count - 1:
            halos[2][1].start()
    for copy in halos[2]:
        copy.wait_recv()

    occ = occ_ref[...]

    def density_part(r, c):
        out = 2.0 * later_product(v2, r, c) - v1[r * EY + c + EY].astype(jnp.float32)
        filtered = out.astype(jnp.bfloat16)
        weighted = (filtered.astype(jnp.float32) * occ).astype(jnp.bfloat16)
        return lax.dot_general(
            weighted, filtered, (((1,), (1,)), ((), ())), preferred_element_type=jnp.float32
        )

    def order(o):
        return [(o + t) % bits for t in range(bits)]

    def part_copy(k, s, o, bit):
        return pltpu.make_async_remote_copy(
            packed.at[k, s, o], arrived.at[k, s, o],
            part_send.at[k, s, o], part_recv.at[k, s, o], device_id={"band": partner(bit)},
        )

    def sent_in(o, t):
        seq = order(o)
        return [
            s for s in range(group)
            if s >> seq[t] & 1 and not any(s >> b & 1 for b in seq[:t])
        ]

    def fold(k, t):
        for o in range(pairs):
            bit = order(o)[t]
            for s in sent_in(o, t):
                part_copy(k, s, o, bit).wait_recv()
                kept = s - (1 << bit)
                packed[k, kept, o] = (
                    packed[k, kept, o].astype(jnp.float32) + arrived[k, s, o].astype(jnp.float32)
                ).astype(jnp.bfloat16)
            if t + 1 < bits:
                for s in sent_in(o, t + 1):
                    part_copy(k, s, o, order(o)[t + 1]).start()

    def row_at(k):
        return (my_row + 1 + k) % row_count

    def cross_copy(k):
        return pltpu.make_async_remote_copy(
            packed.at[k, 0], crossed.at[k], cross_send.at[k], cross_recv.at[k],
            device_id={"band": row_at(k) * group + mine},
        )

    for k in range(row_count):
        r = row_at(k)

        def slot_body(i, carry, k=k, r=r):
            s = group - 1 - i
            owner = 0
            for b in range(bits):
                owner = owner + ((s // (1 << b) + mine // (1 << b)) % 2) * (1 << b)
            for o in range(pairs):
                c = owner * owned + 2 * o
                both = pack_pair(density_part(r, c), density_part(r, c + 1))
                packed[k, s, o] = both.astype(jnp.bfloat16)
            for o in range(pairs):
                bit = order(o)[0]

                @pl.when((s // (1 << bit)) % 2 == 1)
                def _():
                    part_copy(k, s, o, bit).start()

            if k > 0:
                @pl.when(i == group // 2 - 1)
                def _():
                    fold(k - 1, 0)

            return carry

        lax.fori_loop(0, group, slot_body, 0)
        if k > 0:
            for t in range(1, bits):
                fold(k - 1, t)
            cross_copy(k - 1).start()

    last = row_count - 1
    for t in range(bits):
        fold(last, t)
    for k in range(last):
        cross_copy(k).wait_recv()
    for o in range(pairs):
        total = packed[last, 0, o].astype(jnp.float32)
        for k in range(last):
            total = total + crossed[k, o].astype(jnp.float32)
        first, second = unpack_pair(total / total_bands)
        out_ref[2 * o] = first
        out_ref[2 * o + 1] = second

    for up, down in halos:
        up.wait_send()
        down.wait_send()
    for k in range(row_count):
        for o in range(pairs):
            for t in range(bits):
                for s in sent_in(o, t):
                    part_copy(k, s, o, order(o)[t]).wait_send()
        if k < last:
            cross_copy(k).wait_send()


def local(strips, bands, coeffs, hamiltonian, adjacency, occupation):
    elems, basis, columns = coeffs.shape
    row_count = elems // EY
    group = bands // row_count
    owned = EY // group
    assert group * row_count == bands and group * owned == EY and group & (group - 1) == 0
    assert owned % 2 == 0 and row_count >= 3 and strips >= 2 and columns == basis
    field = pltpu.VMEM((elems + 2 * EY, basis, columns), jnp.bfloat16)
    block = (owned // 2, basis + PAD, basis)
    dma = pltpu.SemaphoreType.DMA
    flops = 2 * elems * basis * basis * columns * 16
    return pl.pallas_call(
        functools.partial(kernel, strips, bands, float(columns * bands)),
        out_shape=jax.ShapeDtypeStruct((owned, basis, basis), jnp.float32),
        in_specs=[
            pl.BlockSpec(memory_space=pltpu.SMEM),
            pl.BlockSpec(memory_space=pltpu.VMEM),
            pl.BlockSpec(memory_space=pl.ANY),
            pl.BlockSpec(memory_space=pl.ANY),
        ],
        out_specs=pl.BlockSpec(memory_space=pltpu.VMEM),
        scratch_shapes=[
            pltpu.VMEM((elems * 5, basis, basis), jnp.bfloat16),
            field, field, field,
            pltpu.VMEM((row_count, group) + block, jnp.bfloat16),
            pltpu.VMEM((row_count, group) + block, jnp.bfloat16),
            pltpu.VMEM((row_count - 1,) + block, jnp.bfloat16),
            pltpu.SMEM((elems * 5,), jnp.int32),
            dma((row_count,)), dma, dma((6,)), dma((6,)),
            dma((row_count, group, owned // 2)), dma((row_count, group, owned // 2)),
            dma((row_count - 1,)), dma((row_count - 1,)),
        ],
        compiler_params=pltpu.CompilerParams(
            collective_id=0, has_side_effects=True, vmem_limit_bytes=48 * MIB
        ),
        cost_estimate=pl.CostEstimate(
            flops=flops, bytes_accessed=2 * elems * basis * (5 * basis + columns), transcendentals=0
        ),
        name="chebyshev_density",
    )(
        adjacency,
        occupation.reshape(1, columns),
        coeffs,
        hamiltonian.reshape(elems * 5, basis, basis),
    )


def solution(mesh):
    return jax.shard_map(
        functools.partial(local, mesh.shape["strip"], mesh.shape["band"]),
        mesh=mesh,
        in_specs=(
            P("strip", None, "band"),
            P("strip", None, None, None),
            P("strip", None),
            P("band"),
        ),
        out_specs=P(("strip", "band"), None, None),
        check_vma=False,
    )
```

```python
import functools
import jax
import jax.numpy as jnp
from jax import lax
from jax.experimental import pallas as pl
from jax.experimental.pallas import tpu as pltpu
from jax.sharding import PartitionSpec as P

EY = 16
PAD = 16
MIB = 1 << 20


def lanes(shape):
    return lax.broadcasted_iota(jnp.int32, shape, 1)


def rows(shape):
    return lax.broadcasted_iota(jnp.int32, shape, 0)


def pack_pair(first, second):
    half = first.shape[0] // 2
    left = lanes((half, 2 * half)) < half
    lane = jnp.where(left, lanes(left.shape), lanes(left.shape) - half)
    row = rows(left.shape)
    blocks_1 = jnp.where(left, first[:half], first[half:])
    blocks_2 = jnp.where(left, second[:half], second[half:])
    triangles = jnp.where(row >= lane, blocks_1, blocks_2)
    corners = jnp.where(left, second[half:], first[:half])
    diagonal = jnp.sum(jnp.where(row == lane, blocks_2, 0.0), axis=0, keepdims=True)
    return jnp.concatenate(
        [triangles, corners, jnp.broadcast_to(diagonal, (PAD, 2 * half))], axis=0
    )


def unpack_pair(packed):
    nb = packed.shape[1]
    half = nb // 2
    triangles, corners, diagonal = packed[:half], packed[half:nb], packed[nb:nb + 1]
    left = lanes((half, nb)) < half
    i, j = rows((nb, nb)), lanes((nb, nb))
    same = (i < half) == (j < half)
    wide_1 = jnp.concatenate([jnp.where(left, triangles, corners), triangles], axis=0)
    held_1 = (same & (i >= j)) | ((i < half) & (j >= half))
    first = jnp.where(held_1, wide_1, wide_1.T)
    wide_2 = jnp.concatenate([triangles, jnp.where(left, corners, triangles)], axis=0)
    held_2 = (same & (i < j)) | ((i >= half) & (j < half))
    second = jnp.where(held_2, wide_2, wide_2.T)
    second = jnp.where(i == j, jnp.broadcast_to(diagonal, (nb, nb)), second)
    return first, second


def kernel(
    strips, bands, total_bands,
    adj_hbm, occ_hbm, coeffs_hbm, ham_hbm, out_ref,
    ham, v0, v0_first, v0_last, v1, v2, packed, arrived, crossed, adj_ref, occ_ref, table, slots,
    ham_sem, own_sem, halo_send, halo_recv, part_send, part_recv, cross_send, cross_recv,
):
    elems = coeffs_hbm.shape[0]
    row_count = elems // EY
    group = bands // row_count
    bits = group.bit_length() - 1
    owned = EY // group
    pairs = owned // 2
    strip = lax.axis_index("strip")
    band = lax.axis_index("band")
    my_row, mine = band // group, band % group
    above, below = (strip + strips - 1) % strips, (strip + 1) % strips

    def partner(bit):
        step = 1 << bit
        return band + step * (1 - 2 * ((band // step) % 2))

    adj_copy = pltpu.make_async_copy(adj_hbm, adj_ref, own_sem.at[0])
    occ_copy = pltpu.make_async_copy(occ_hbm, occ_ref, own_sem.at[1])
    own_copy = pltpu.make_async_copy(coeffs_hbm, v0, own_sem.at[2])
    table_copy = pltpu.make_async_copy(table, slots, own_sem.at[3])
    adj_copy.start()
    own_copy.start()
    per_row = EY * 5
    ham_copies = [
        pltpu.make_async_copy(
            ham_hbm.at[pl.ds(r * per_row, per_row)], ham.at[pl.ds(r * per_row, per_row)], ham_sem.at[r]
        )
        for r in range(row_count)
    ]
    last = row_count - 1
    first_order = list(range(1, last)) + [0, last]
    row_order = [1, 0, last] + list(range(2, last))
    for r in first_order:
        ham_copies[r].start()
    occ_copy.start()

    barrier = pltpu.get_barrier_semaphore()
    greeted = 0
    for target in [above] if strips == 2 else [above, below]:
        pl.semaphore_signal(barrier, inc=1, device_id={"strip": target})
        greeted += 1
    for bit in range(bits):
        pl.semaphore_signal(barrier, inc=1, device_id={"band": partner(bit)})
        greeted += 1
    for away in range(1, row_count):
        pl.semaphore_signal(
            barrier, inc=1, device_id={"band": ((my_row + away) % row_count) * group + mine}
        )
        greeted += 1

    adj_copy.wait()
    sheet_rows = row_count * strips
    a = adj_ref[...]
    places = lax.rem(lax.div(a, EY) - strip * row_count + sheet_rows, sheet_rows) * EY + lax.rem(a, EY)
    here = lanes((1, elems))
    line, col = lax.div(here, EY), lax.rem(here, EY)
    wanted = [
        here,
        lax.rem(line + sheet_rows - 1, sheet_rows) * EY + col,
        lax.rem(line + 1, sheet_rows) * EY + col,
        line * EY + lax.rem(col + EY - 1, EY),
        line * EY + lax.rem(col + 1, EY),
    ]
    for d in range(5):
        slot = here * 0
        for j in range(1, 5):
            slot = slot + jnp.where(places[j:j + 1] == wanted[d], j, 0)
        table[d:d + 1, :elems] = jnp.minimum(slot, 4)
        table[8 + d:9 + d, :elems] = jnp.minimum(places[d:d + 1], elems - 1)
    table_copy.start()
    pl.semaphore_wait(barrier, greeted)

    def halo(field, source, shift, first, final):
        up = pltpu.make_async_remote_copy(
            source.at[pl.ds(shift, EY)], final,
            halo_send.at[2 * field], halo_recv.at[2 * field], device_id={"strip": above},
        )
        down = pltpu.make_async_remote_copy(
            source.at[pl.ds(shift + elems - EY, EY)], first,
            halo_send.at[2 * field + 1], halo_recv.at[2 * field + 1], device_id={"strip": below},
        )
        return up, down

    ends = [(v.at[pl.ds(0, EY)], v.at[pl.ds(EY + elems, EY)]) for v in (v1, v2)]
    halos = [
        halo(0, coeffs_hbm, 0, v0_first, v0_last), halo(1, v1, EY, *ends[0]), halo(2, v2, EY, *ends[1])
    ]
    for copy in halos[0]:
        copy.start()

    def product(blocks, fields):
        return jnp.dot(
            jnp.concatenate(blocks, axis=1), jnp.concatenate(fields, axis=0),
            preferred_element_type=jnp.float32,
        )

    def inner_element(r, c):
        e = r * EY + c
        out = product(
            [ham[e * 5 + j] for j in range(5)], [v0[slots[8 + j, e]] for j in range(5)]
        )
        v1[e + EY] = out.astype(jnp.bfloat16)

    def blocks_of(e):
        return [ham[e * 5 + slots[d, e]] for d in range(5)]

    def outer_element(r, c):
        e = r * EY + c
        line = r * EY
        fields = [
            v0[e],
            v0_first[c] if r == 0 else v0[e - EY],
            v0_last[c] if r == last else v0[e + EY],
            v0[line + lax.rem(c + EY - 1, EY)], v0[line + lax.rem(c + 1, EY)],
        ]
        v1[e + EY] = product(blocks_of(e), fields).astype(jnp.bfloat16)

    def later_product(ref, r, c):
        e = r * EY + c
        here = e + EY
        line = (r + 1) * EY
        fields = [
            ref[here], ref[here - EY], ref[here + EY],
            ref[line + lax.rem(c + EY - 1, EY)], ref[line + lax.rem(c + 1, EY)],
        ]
        return product(blocks_of(e), fields)

    def second_element(r, c):
        e = r * EY + c
        out = 2.0 * later_product(v1, r, c) - v0[e].astype(jnp.float32)
        v2[e + EY] = out.astype(jnp.bfloat16)

    STEP = 4

    def one_row(element, r):
        def body(g, carry):
            for m in range(STEP):
                element(r, g * STEP + m)
            return carry

        lax.fori_loop(0, EY // STEP, body, 0)

    own_copy.wait()
    table_copy.wait()
    for r in first_order[:-2]:
        ham_copies[r].wait()
        one_row(inner_element, r)
    for r in (0, last):
        ham_copies[r].wait()
    for copy in halos[0]:
        copy.wait_recv()
    for r in (0, last):
        one_row(outer_element, r)
        if r == 0:
            halos[1][0].start()
        if r == row_count - 1:
            halos[1][1].start()
    for r in row_order:
        if r == 0:
            halos[1][1].wait_recv()
        if r == row_count - 1:
            halos[1][0].wait_recv()
        one_row(second_element, r)
        if r == 0:
            halos[2][0].start()
        if r == row_count - 1:
            halos[2][1].start()
    for copy in halos[2]:
        copy.wait_recv()

    occ_copy.wait()
    occ = occ_ref[...]

    def density_part(r, c):
        out = 2.0 * later_product(v2, r, c) - v1[r * EY + c + EY].astype(jnp.float32)
        filtered = out.astype(jnp.bfloat16)
        weighted = (filtered.astype(jnp.float32) * occ).astype(jnp.bfloat16)
        return lax.dot_general(
            weighted, filtered, (((1,), (1,)), ((), ())), preferred_element_type=jnp.float32
        )

    def order(o):
        return [(o + t) % bits for t in range(bits)]

    def part_copy(k, s, o, bit):
        return pltpu.make_async_remote_copy(
            packed.at[k, s, o], arrived.at[k, s, o],
            part_send.at[k, s, o], part_recv.at[k, s, o], device_id={"band": partner(bit)},
        )

    def sent_in(o, t):
        seq = order(o)
        return [
            s for s in range(group)
            if s >> seq[t] & 1 and not any(s >> b & 1 for b in seq[:t])
        ]

    def fold(k, t):
        for o in range(pairs):
            bit = order(o)[t]
            for s in sent_in(o, t):
                part_copy(k, s, o, bit).wait_recv()
                kept = s - (1 << bit)
                packed[k, kept, o] = (
                    packed[k, kept, o].astype(jnp.float32) + arrived[k, s, o].astype(jnp.float32)
                ).astype(jnp.bfloat16)
            if t + 1 < bits:
                for s in sent_in(o, t + 1):
                    part_copy(k, s, o, order(o)[t + 1]).start()

    def row_at(k):
        return (my_row + 1 + k) % row_count

    def cross_copy(k):
        return pltpu.make_async_remote_copy(
            packed.at[k, 0], crossed.at[k], cross_send.at[k], cross_recv.at[k],
            device_id={"band": row_at(k) * group + mine},
        )

    for k in range(row_count):
        r = row_at(k)

        def slot_body(i, carry, k=k, r=r):
            s = group - 1 - i
            owner = 0
            for b in range(bits):
                owner = owner + ((s // (1 << b) + mine // (1 << b)) % 2) * (1 << b)
            for o in range(pairs):
                c = owner * owned + 2 * o
                both = pack_pair(density_part(r, c), density_part(r, c + 1))
                packed[k, s, o] = both.astype(jnp.bfloat16)
            for o in range(pairs):
                bit = order(o)[0]

                @pl.when((s // (1 << bit)) % 2 == 1)
                def _():
                    part_copy(k, s, o, bit).start()

            if k > 0:
                @pl.when(i == group // 2 - 1)
                def _():
                    fold(k - 1, 0)

            return carry

        lax.fori_loop(0, group, slot_body, 0)
        if k > 0:
            for t in range(1, bits):
                fold(k - 1, t)
            cross_copy(k - 1).start()

    for t in range(bits):
        fold(last, t)
    for k in range(last):
        cross_copy(k).wait_recv()
    for o in range(pairs):
        total = packed[last, 0, o].astype(jnp.float32)
        for k in range(last):
            total = total + crossed[k, o].astype(jnp.float32)
        first, second = unpack_pair(total / total_bands)
        out_ref[2 * o] = first
        out_ref[2 * o + 1] = second

    for up, down in halos:
        up.wait_send()
        down.wait_send()
    for k in range(row_count):
        for o in range(pairs):
            for t in range(bits):
                for s in sent_in(o, t):
                    part_copy(k, s, o, order(o)[t]).wait_send()
        if k < last:
            cross_copy(k).wait_send()


def local(strips, bands, coeffs, hamiltonian, adjacency, occupation):
    elems, basis, columns = coeffs.shape
    row_count = elems // EY
    group = bands // row_count
    owned = EY // group
    assert group * row_count == bands and group * owned == EY and group & (group - 1) == 0
    assert owned % 2 == 0 and row_count >= 3 and strips >= 2 and columns == basis
    edge = pltpu.VMEM((EY, basis, columns), jnp.bfloat16)
    own = pltpu.VMEM((elems, basis, columns), jnp.bfloat16)
    field = pltpu.VMEM((elems + 2 * EY, basis, columns), jnp.bfloat16)
    block = (owned // 2, basis + PAD, basis)
    wide = -(-elems // 128) * 128
    dma = pltpu.SemaphoreType.DMA
    flops = 2 * elems * basis * basis * columns * 16
    return pl.pallas_call(
        functools.partial(kernel, strips, bands, float(columns * bands)),
        out_shape=jax.ShapeDtypeStruct((owned, basis, basis), jnp.float32),
        in_specs=[
            pl.BlockSpec(memory_space=pl.ANY),
            pl.BlockSpec(memory_space=pl.ANY),
            pl.BlockSpec(memory_space=pl.ANY),
            pl.BlockSpec(memory_space=pl.ANY),
        ],
        out_specs=pl.BlockSpec(memory_space=pltpu.VMEM),
        scratch_shapes=[
            pltpu.VMEM((elems * 5, basis, basis), jnp.bfloat16),
            own, edge, edge, field, field,
            pltpu.VMEM((row_count, group) + block, jnp.bfloat16),
            pltpu.VMEM((row_count, group) + block, jnp.bfloat16),
            pltpu.VMEM((row_count - 1,) + block, jnp.bfloat16),
            pltpu.VMEM((5, elems), jnp.int32),
            pltpu.VMEM((1, columns), jnp.float32),
            pltpu.VMEM((16, wide), jnp.int32),
            pltpu.SMEM((16, wide), jnp.int32),
            dma((row_count,)), dma((4,)), dma((6,)), dma((6,)),
            dma((row_count, group, owned // 2)), dma((row_count, group, owned // 2)),
            dma((row_count - 1,)), dma((row_count - 1,)),
        ],
        compiler_params=pltpu.CompilerParams(
            collective_id=0, has_side_effects=True, vmem_limit_bytes=63 * MIB
        ),
        cost_estimate=pl.CostEstimate(
            flops=flops, bytes_accessed=2 * elems * basis * (5 * basis + columns), transcendentals=0
        ),
        name="chebyshev_density",
    )(
        adjacency.T,
        occupation.reshape(1, columns),
        coeffs,
        hamiltonian.reshape(elems * 5, basis, basis),
    )


def solution(mesh):
    return jax.shard_map(
        functools.partial(local, mesh.shape["strip"], mesh.shape["band"]),
        mesh=mesh,
        in_specs=(
            P("strip", None, "band"),
            P("strip", None, None, None),
            P("strip", None),
            P("band"),
        ),
        out_specs=P(("strip", "band"), None, None),
        check_vma=False,
    )
```

```python
import functools
import jax
import jax.numpy as jnp
from jax import lax
from jax.experimental import pallas as pl
from jax.experimental.pallas import tpu as pltpu
from jax.sharding import PartitionSpec as P

EY = 16
PAD = 16
MIB = 1 << 20


def lanes(shape):
    return lax.broadcasted_iota(jnp.int32, shape, 1)


def rows(shape):
    return lax.broadcasted_iota(jnp.int32, shape, 0)


def pack_pair(first, second):
    half = first.shape[0] // 2
    left = lanes((half, 2 * half)) < half
    lane = jnp.where(left, lanes(left.shape), lanes(left.shape) - half)
    row = rows(left.shape)
    blocks_1 = jnp.where(left, first[:half], first[half:])
    blocks_2 = jnp.where(left, second[:half], second[half:])
    triangles = jnp.where(row >= lane, blocks_1, blocks_2)
    corners = jnp.where(left, second[half:], first[:half])
    diagonal = jnp.sum(jnp.where(row == lane, blocks_2, 0.0), axis=0, keepdims=True)
    return jnp.concatenate(
        [triangles, corners, jnp.broadcast_to(diagonal, (PAD, 2 * half))], axis=0
    )


def unpack_pair(packed):
    nb = packed.shape[1]
    half = nb // 2
    triangles, corners, diagonal = packed[:half], packed[half:nb], packed[nb:nb + 1]
    left = lanes((half, nb)) < half
    i, j = rows((nb, nb)), lanes((nb, nb))
    same = (i < half) == (j < half)
    wide_1 = jnp.concatenate([jnp.where(left, triangles, corners), triangles], axis=0)
    held_1 = (same & (i >= j)) | ((i < half) & (j >= half))
    first = jnp.where(held_1, wide_1, wide_1.T)
    wide_2 = jnp.concatenate([triangles, jnp.where(left, corners, triangles)], axis=0)
    held_2 = (same & (i < j)) | ((i >= half) & (j < half))
    second = jnp.where(held_2, wide_2, wide_2.T)
    second = jnp.where(i == j, jnp.broadcast_to(diagonal, (nb, nb)), second)
    return first, second


def kernel(
    strips, bands, total_bands,
    adj_hbm, occ_hbm, coeffs_hbm, ham_hbm, out_ref,
    ham, v0, v0_first, v0_last, v1, v2, packed, arrived, crossed, adj_ref, occ_ref, table, slots,
    ham_sem, own_sem, halo_send, halo_recv, part_send, part_recv, cross_send, cross_recv,
):
    elems = coeffs_hbm.shape[0]
    row_count = elems // EY
    group = bands // row_count
    bits = group.bit_length() - 1
    owned = EY // group
    pairs = owned // 2
    strip = lax.axis_index("strip")
    band = lax.axis_index("band")
    my_row, mine = band // group, band % group
    above, below = (strip + strips - 1) % strips, (strip + 1) % strips

    def partner(bit):
        step = 1 << bit
        return band + step * (1 - 2 * ((band // step) % 2))

    adj_copy = pltpu.make_async_copy(adj_hbm, adj_ref, own_sem.at[0])
    occ_copy = pltpu.make_async_copy(occ_hbm, occ_ref, own_sem.at[1])
    own_copy = pltpu.make_async_copy(coeffs_hbm, v0, own_sem.at[2])
    table_copy = pltpu.make_async_copy(table, slots, own_sem.at[3])
    adj_copy.start()
    own_copy.start()
    per_row = EY * 5
    ham_copies = [
        pltpu.make_async_copy(
            ham_hbm.at[pl.ds(r * per_row, per_row)], ham.at[pl.ds(r * per_row, per_row)], ham_sem.at[r]
        )
        for r in range(row_count)
    ]
    last = row_count - 1
    first_order = list(range(1, last)) + [0, last]
    row_order = [1, 0, last] + list(range(2, last))
    for r in first_order:
        ham_copies[r].start()
    occ_copy.start()

    barrier = pltpu.get_barrier_semaphore()
    greeted = 0
    for target in [above] if strips == 2 else [above, below]:
        pl.semaphore_signal(barrier, inc=1, device_id={"strip": target})
        greeted += 1
    for bit in range(bits):
        pl.semaphore_signal(barrier, inc=1, device_id={"band": partner(bit)})
        greeted += 1
    for away in range(1, row_count):
        pl.semaphore_signal(
            barrier, inc=1, device_id={"band": ((my_row + away) % row_count) * group + mine}
        )
        greeted += 1

    adj_copy.wait()
    sheet_rows = row_count * strips
    a = adj_ref[...]
    places = lax.rem(lax.div(a, EY) - strip * row_count + sheet_rows, sheet_rows) * EY + lax.rem(a, EY)
    here = lanes((1, elems))
    line, col = lax.div(here, EY), lax.rem(here, EY)
    wanted = [
        here,
        lax.rem(line + sheet_rows - 1, sheet_rows) * EY + col,
        lax.rem(line + 1, sheet_rows) * EY + col,
        line * EY + lax.rem(col + EY - 1, EY),
        line * EY + lax.rem(col + 1, EY),
    ]
    for d in range(5):
        slot = here * 0
        for j in range(1, 5):
            slot = slot + jnp.where(places[j:j + 1] == wanted[d], j, 0)
        table[d:d + 1, :elems] = jnp.minimum(slot, 4)
        table[8 + d:9 + d, :elems] = jnp.minimum(places[d:d + 1], elems - 1)
    table_copy.start()
    pl.semaphore_wait(barrier, greeted)

    def halo(field, source, shift, first, final):
        up = pltpu.make_async_remote_copy(
            source.at[pl.ds(shift, EY)], final,
            halo_send.at[2 * field], halo_recv.at[2 * field], device_id={"strip": above},
        )
        down = pltpu.make_async_remote_copy(
            source.at[pl.ds(shift + elems - EY, EY)], first,
            halo_send.at[2 * field + 1], halo_recv.at[2 * field + 1], device_id={"strip": below},
        )
        return up, down

    ends = [(v.at[pl.ds(0, EY)], v.at[pl.ds(EY + elems, EY)]) for v in (v1, v2)]
    halos = [
        halo(0, coeffs_hbm, 0, v0_first, v0_last), halo(1, v1, EY, *ends[0]), halo(2, v2, EY, *ends[1])
    ]
    for copy in halos[0]:
        copy.start()

    def product(blocks, fields):
        return jnp.dot(
            jnp.concatenate(blocks, axis=1), jnp.concatenate(fields, axis=0),
            preferred_element_type=jnp.float32,
        )

    def inner_element(r, c):
        e = r * EY + c
        out = product(
            [ham[e * 5 + j] for j in range(5)], [v0[slots[8 + j, e]] for j in range(5)]
        )
        v1[e + EY] = out.astype(jnp.bfloat16)

    def blocks_of(e):
        return [ham[e * 5 + slots[d, e]] for d in range(5)]

    def outer_element(r, c):
        e = r * EY + c
        line = r * EY
        fields = [
            v0[e],
            v0_first[c] if r == 0 else v0[e - EY],
            v0_last[c] if r == last else v0[e + EY],
            v0[line + lax.rem(c + EY - 1, EY)], v0[line + lax.rem(c + 1, EY)],
        ]
        v1[e + EY] = product(blocks_of(e), fields).astype(jnp.bfloat16)

    def later_product(ref, r, c):
        e = r * EY + c
        here = e + EY
        line = (r + 1) * EY
        fields = [
            ref[here], ref[here - EY], ref[here + EY],
            ref[line + lax.rem(c + EY - 1, EY)], ref[line + lax.rem(c + 1, EY)],
        ]
        return product(blocks_of(e), fields)

    def second_element(r, c):
        e = r * EY + c
        out = 2.0 * later_product(v1, r, c) - v0[e].astype(jnp.float32)
        v2[e + EY] = out.astype(jnp.bfloat16)

    STEP = 16

    def one_row(element, r):
        def body(g, carry):
            for m in range(STEP):
                element(r, g * STEP + m)
            return carry

        lax.fori_loop(0, EY // STEP, body, 0)

    own_copy.wait()
    table_copy.wait()
    for r in first_order[:-2]:
        ham_copies[r].wait()
        one_row(inner_element, r)
    for r in (0, last):
        ham_copies[r].wait()
    for copy in halos[0]:
        copy.wait_recv()
    for r in (0, last):
        one_row(outer_element, r)
        if r == 0:
            halos[1][0].start()
        if r == row_count - 1:
            halos[1][1].start()
    for r in row_order:
        if r == 0:
            halos[1][1].wait_recv()
        if r == row_count - 1:
            halos[1][0].wait_recv()
        one_row(second_element, r)
        if r == 0:
            halos[2][0].start()
        if r == row_count - 1:
            halos[2][1].start()
    for copy in halos[2]:
        copy.wait_recv()

    occ_copy.wait()
    occ = occ_ref[...]

    def density_part(r, c):
        out = 2.0 * later_product(v2, r, c) - v1[r * EY + c + EY].astype(jnp.float32)
        filtered = out.astype(jnp.bfloat16)
        weighted = (filtered.astype(jnp.float32) * occ).astype(jnp.bfloat16)
        return lax.dot_general(
            weighted, filtered, (((1,), (1,)), ((), ())), preferred_element_type=jnp.float32
        )

    def order(o):
        return [(o + t) % bits for t in range(bits)]

    def part_copy(k, s, o, bit):
        return pltpu.make_async_remote_copy(
            packed.at[k, s, o], arrived.at[k, s, o],
            part_send.at[k, s, o], part_recv.at[k, s, o], device_id={"band": partner(bit)},
        )

    def sent_in(o, t):
        seq = order(o)
        return [
            s for s in range(group)
            if s >> seq[t] & 1 and not any(s >> b & 1 for b in seq[:t])
        ]

    def fold(k, t):
        for o in range(pairs):
            bit = order(o)[t]
            for s in sent_in(o, t):
                part_copy(k, s, o, bit).wait_recv()
                kept = s - (1 << bit)
                packed[k, kept, o] = (
                    packed[k, kept, o].astype(jnp.float32) + arrived[k, s, o].astype(jnp.float32)
                ).astype(jnp.bfloat16)
            if t + 1 < bits:
                for s in sent_in(o, t + 1):
                    part_copy(k, s, o, order(o)[t + 1]).start()

    def row_at(k):
        return (my_row + 1 + k) % row_count

    def cross_copy(k):
        return pltpu.make_async_remote_copy(
            packed.at[k, 0], crossed.at[k], cross_send.at[k], cross_recv.at[k],
            device_id={"band": row_at(k) * group + mine},
        )

    for k in range(row_count):
        r = row_at(k)

        for i in range(group):
            s = group - 1 - i
            owner = 0
            for b in range(bits):
                owner = owner + ((s // (1 << b) + mine // (1 << b)) % 2) * (1 << b)
            for o in range(pairs):
                c = owner * owned + 2 * o
                both = pack_pair(density_part(r, c), density_part(r, c + 1))
                packed[k, s, o] = both.astype(jnp.bfloat16)
            for o in range(pairs):
                if s in sent_in(o, 0):
                    part_copy(k, s, o, order(o)[0]).start()
            if k > 0 and i == group // 2 - 1:
                fold(k - 1, 0)
        if k > 0:
            for t in range(1, bits):
                fold(k - 1, t)
            cross_copy(k - 1).start()

    for t in range(bits):
        fold(last, t)
    for k in range(last):
        cross_copy(k).wait_recv()
    for o in range(pairs):
        total = packed[last, 0, o].astype(jnp.float32)
        for k in range(last):
            total = total + crossed[k, o].astype(jnp.float32)
        first, second = unpack_pair(total / total_bands)
        out_ref[2 * o] = first
        out_ref[2 * o + 1] = second

    for up, down in halos:
        up.wait_send()
        down.wait_send()
    for k in range(row_count):
        for o in range(pairs):
            for t in range(bits):
                for s in sent_in(o, t):
                    part_copy(k, s, o, order(o)[t]).wait_send()
        if k < last:
            cross_copy(k).wait_send()


def local(strips, bands, coeffs, hamiltonian, adjacency, occupation):
    elems, basis, columns = coeffs.shape
    row_count = elems // EY
    group = bands // row_count
    owned = EY // group
    assert group * row_count == bands and group * owned == EY and group & (group - 1) == 0
    assert owned % 2 == 0 and row_count >= 3 and strips >= 2 and columns == basis
    edge = pltpu.VMEM((EY, basis, columns), jnp.bfloat16)
    own = pltpu.VMEM((elems, basis, columns), jnp.bfloat16)
    field = pltpu.VMEM((elems + 2 * EY, basis, columns), jnp.bfloat16)
    block = (owned // 2, basis + PAD, basis)
    wide = -(-elems // 128) * 128
    dma = pltpu.SemaphoreType.DMA
    flops = 2 * elems * basis * basis * columns * 16
    return pl.pallas_call(
        functools.partial(kernel, strips, bands, float(columns * bands)),
        out_shape=jax.ShapeDtypeStruct((owned, basis, basis), jnp.float32),
        in_specs=[
            pl.BlockSpec(memory_space=pl.ANY),
            pl.BlockSpec(memory_space=pl.ANY),
            pl.BlockSpec(memory_space=pl.ANY),
            pl.BlockSpec(memory_space=pl.ANY),
        ],
        out_specs=pl.BlockSpec(memory_space=pltpu.VMEM),
        scratch_shapes=[
            pltpu.VMEM((elems * 5, basis, basis), jnp.bfloat16),
            own, edge, edge, field, field,
            pltpu.VMEM((row_count, group) + block, jnp.bfloat16),
            pltpu.VMEM((row_count, group) + block, jnp.bfloat16),
            pltpu.VMEM((row_count - 1,) + block, jnp.bfloat16),
            pltpu.VMEM((5, elems), jnp.int32),
            pltpu.VMEM((1, columns), jnp.float32),
            pltpu.VMEM((16, wide), jnp.int32),
            pltpu.SMEM((16, wide), jnp.int32),
            dma((row_count,)), dma((4,)), dma((6,)), dma((6,)),
            dma((row_count, group, owned // 2)), dma((row_count, group, owned // 2)),
            dma((row_count - 1,)), dma((row_count - 1,)),
        ],
        compiler_params=pltpu.CompilerParams(
            collective_id=0, has_side_effects=True, vmem_limit_bytes=62 * MIB
        ),
        cost_estimate=pl.CostEstimate(
            flops=flops, bytes_accessed=2 * elems * basis * (5 * basis + columns), transcendentals=0
        ),
        name="chebyshev_density",
    )(
        adjacency.T,
        occupation.reshape(1, columns),
        coeffs,
        hamiltonian.reshape(elems * 5, basis, basis),
    )


def solution(mesh):
    return jax.shard_map(
        functools.partial(local, mesh.shape["strip"], mesh.shape["band"]),
        mesh=mesh,
        in_specs=(
            P("strip", None, "band"),
            P("strip", None, None, None),
            P("strip", None),
            P("band"),
        ),
        out_specs=P(("strip", "band"), None, None),
        check_vma=False,
    )
```

```python
import functools
import jax
import jax.numpy as jnp
from jax import lax
from jax.experimental import pallas as pl
from jax.experimental.pallas import tpu as pltpu
from jax.sharding import PartitionSpec as P

EY = 16
PAD = 16
MIB = 1 << 20


def lanes(shape):
    return lax.broadcasted_iota(jnp.int32, shape, 1)


def rows(shape):
    return lax.broadcasted_iota(jnp.int32, shape, 0)


def pack_pair(first, second):
    half = first.shape[0] // 2
    left = lanes((half, 2 * half)) < half
    lane = jnp.where(left, lanes(left.shape), lanes(left.shape) - half)
    row = rows(left.shape)
    blocks_1 = jnp.where(left, first[:half], first[half:])
    blocks_2 = jnp.where(left, second[:half], second[half:])
    triangles = jnp.where(row >= lane, blocks_1, blocks_2)
    corners = jnp.where(left, second[half:], first[:half])
    diagonal = jnp.sum(jnp.where(row == lane, blocks_2, 0.0), axis=0, keepdims=True)
    return jnp.concatenate(
        [triangles, corners, jnp.broadcast_to(diagonal, (PAD, 2 * half))], axis=0
    )


def unpack_pair(packed):
    nb = packed.shape[1]
    half = nb // 2
    triangles, corners, diagonal = packed[:half], packed[half:nb], packed[nb:nb + 1]
    left = lanes((half, nb)) < half
    i, j = rows((nb, nb)), lanes((nb, nb))
    same = (i < half) == (j < half)
    wide_1 = jnp.concatenate([jnp.where(left, triangles, corners), triangles], axis=0)
    held_1 = (same & (i >= j)) | ((i < half) & (j >= half))
    first = jnp.where(held_1, wide_1, wide_1.T)
    wide_2 = jnp.concatenate([triangles, jnp.where(left, corners, triangles)], axis=0)
    held_2 = (same & (i < j)) | ((i >= half) & (j < half))
    second = jnp.where(held_2, wide_2, wide_2.T)
    second = jnp.where(i == j, jnp.broadcast_to(diagonal, (nb, nb)), second)
    return first, second


def kernel(
    strips, bands, total_bands,
    adj_hbm, occ_hbm, coeffs_hbm, ham_hbm, out_ref,
    ham, v0, v0_first, v0_last, v1, v2, packed, arrived, crossed, adj_ref, occ_ref, table, slots,
    ham_sem, own_sem, halo_send, halo_recv, part_send, part_recv, cross_send, cross_recv,
):
    elems = coeffs_hbm.shape[0]
    row_count = elems // EY
    group = bands // row_count
    bits = group.bit_length() - 1
    owned = EY // group
    pairs = owned // 2
    strip = lax.axis_index("strip")
    band = lax.axis_index("band")
    my_row, mine = band // group, band % group
    above, below = (strip + strips - 1) % strips, (strip + 1) % strips

    def partner(bit):
        step = 1 << bit
        return band + step * (1 - 2 * ((band // step) % 2))

    adj_copy = pltpu.make_async_copy(adj_hbm, adj_ref, own_sem.at[0])
    occ_copy = pltpu.make_async_copy(occ_hbm, occ_ref, own_sem.at[1])
    own_copy = pltpu.make_async_copy(coeffs_hbm, v0, own_sem.at[2])
    table_copy = pltpu.make_async_copy(table, slots, own_sem.at[3])
    adj_copy.start()
    own_copy.start()
    per_row = EY * 5
    ham_copies = [
        pltpu.make_async_copy(
            ham_hbm.at[pl.ds(r * per_row, per_row)], ham.at[pl.ds(r * per_row, per_row)], ham_sem.at[r]
        )
        for r in range(row_count)
    ]
    last = row_count - 1
    first_order = list(range(1, last)) + [0, last]
    row_order = [1, 0, last] + list(range(2, last))
    for r in first_order:
        ham_copies[r].start()
    occ_copy.start()

    barrier = pltpu.get_barrier_semaphore()
    greeted = 0
    for target in [above] if strips == 2 else [above, below]:
        pl.semaphore_signal(barrier, inc=1, device_id={"strip": target})
        greeted += 1
    for bit in range(bits):
        pl.semaphore_signal(barrier, inc=1, device_id={"band": partner(bit)})
        greeted += 1
    for away in range(1, row_count):
        pl.semaphore_signal(
            barrier, inc=1, device_id={"band": ((my_row + away) % row_count) * group + mine}
        )
        greeted += 1

    adj_copy.wait()
    sheet_rows = row_count * strips
    a = adj_ref[...]
    places = lax.rem(lax.div(a, EY) - strip * row_count + sheet_rows, sheet_rows) * EY + lax.rem(a, EY)
    here = lanes((1, elems))
    line, col = lax.div(here, EY), lax.rem(here, EY)
    wanted = [
        here,
        lax.rem(line + sheet_rows - 1, sheet_rows) * EY + col,
        lax.rem(line + 1, sheet_rows) * EY + col,
        line * EY + lax.rem(col + EY - 1, EY),
        line * EY + lax.rem(col + 1, EY),
    ]
    for d in range(5):
        slot = here * 0
        for j in range(1, 5):
            slot = slot + jnp.where(places[j:j + 1] == wanted[d], j, 0)
        table[d:d + 1, :elems] = jnp.minimum(slot, 4)
        table[8 + d:9 + d, :elems] = jnp.minimum(places[d:d + 1], elems - 1)
    table_copy.start()
    pl.semaphore_wait(barrier, greeted)

    def halo(field, source, shift, first, final):
        up = pltpu.make_async_remote_copy(
            source.at[pl.ds(shift, EY)], final,
            halo_send.at[2 * field], halo_recv.at[2 * field], device_id={"strip": above},
        )
        down = pltpu.make_async_remote_copy(
            source.at[pl.ds(shift + elems - EY, EY)], first,
            halo_send.at[2 * field + 1], halo_recv.at[2 * field + 1], device_id={"strip": below},
        )
        return up, down

    ends = [(v.at[pl.ds(0, EY)], v.at[pl.ds(EY + elems, EY)]) for v in (v1, v2)]
    halos = [
        halo(0, coeffs_hbm, 0, v0_first, v0_last), halo(1, v1, EY, *ends[0]), halo(2, v2, EY, *ends[1])
    ]
    for copy in halos[0]:
        copy.start()

    def product(blocks, fields):
        return jnp.dot(
            jnp.concatenate(blocks, axis=1), jnp.concatenate(fields, axis=0),
            preferred_element_type=jnp.float32,
        )

    def inner_element(r, c):
        e = r * EY + c
        out = product(
            [ham[e * 5 + j] for j in range(5)], [v0[slots[8 + j, e]] for j in range(5)]
        )
        v1[e + EY] = out.astype(jnp.bfloat16)

    def blocks_of(e):
        return [ham[e * 5 + slots[d, e]] for d in range(5)]

    def pair_product(e, field, above_of, below_of, line, c):
        first, second = blocks_of(e), blocks_of(e + 1)
        between = product(
            [
                jnp.concatenate([first[0], second[3]], axis=0),
                jnp.concatenate([first[4], second[0]], axis=0),
            ],
            [field[line + c], field[line + c + 1]],
        )
        rest_1 = product(
            first[1:4], [above_of(c), below_of(c), field[line + lax.rem(c + EY - 1, EY)]]
        )
        rest_2 = product(
            [second[1], second[2], second[4]],
            [above_of(c + 1), below_of(c + 1), field[line + lax.rem(c + 2, EY)]],
        )
        return between[:rest_1.shape[0]] + rest_1, between[rest_1.shape[0]:] + rest_2

    def outer_pair(r, c):
        line = r * EY
        pair = pair_product(
            line + c, v0,
            lambda at: v0_first[at] if r == 0 else v0[line - EY + at],
            lambda at: v0_last[at] if r == last else v0[line + EY + at],
            line, c,
        )
        for m in range(2):
            v1[line + c + m + EY] = pair[m].astype(jnp.bfloat16)

    def later_pair(ref, r, c):
        line = (r + 1) * EY
        return pair_product(
            r * EY + c, ref, lambda at: ref[line - EY + at], lambda at: ref[line + EY + at], line, c
        )

    def second_pair(r, c):
        e = r * EY + c
        pair = later_pair(v1, r, c)
        for m in range(2):
            out = 2.0 * pair[m] - v0[e + m].astype(jnp.float32)
            v2[e + m + EY] = out.astype(jnp.bfloat16)

    def one_row(step, element, r):
        for c in range(0, EY, step):
            element(r, c)

    own_copy.wait()
    table_copy.wait()
    for r in first_order[:-2]:
        ham_copies[r].wait()
        one_row(1, inner_element, r)
    for r in (0, last):
        ham_copies[r].wait()
    for copy in halos[0]:
        copy.wait_recv()
    for r in (0, last):
        one_row(2, outer_pair, r)
        if r == 0:
            halos[1][0].start()
        if r == row_count - 1:
            halos[1][1].start()
    for r in row_order:
        if r == 0:
            halos[1][1].wait_recv()
        if r == row_count - 1:
            halos[1][0].wait_recv()
        one_row(2, second_pair, r)
        if r == 0:
            halos[2][0].start()
        if r == row_count - 1:
            halos[2][1].start()
    for copy in halos[2]:
        copy.wait_recv()

    occ_copy.wait()
    occ = occ_ref[...]

    def density_pair(r, c):
        parts = []
        for m, product_m in enumerate(later_pair(v2, r, c)):
            out = 2.0 * product_m - v1[r * EY + c + m + EY].astype(jnp.float32)
            filtered = out.astype(jnp.bfloat16)
            weighted = (filtered.astype(jnp.float32) * occ).astype(jnp.bfloat16)
            parts.append(lax.dot_general(
                weighted, filtered, (((1,), (1,)), ((), ())), preferred_element_type=jnp.float32
            ))
        return parts

    def order(o):
        return [(o + t) % bits for t in range(bits)]

    def part_copy(k, s, o, bit):
        return pltpu.make_async_remote_copy(
            packed.at[k, s, o], arrived.at[k, s, o],
            part_send.at[k, s, o], part_recv.at[k, s, o], device_id={"band": partner(bit)},
        )

    def sent_in(o, t):
        seq = order(o)
        return [
            s for s in range(group)
            if s >> seq[t] & 1 and not any(s >> b & 1 for b in seq[:t])
        ]

    def fold(k, t):
        for o in range(pairs):
            bit = order(o)[t]
            for s in sent_in(o, t):
                part_copy(k, s, o, bit).wait_recv()
                kept = s - (1 << bit)
                packed[k, kept, o] = (
                    packed[k, kept, o].astype(jnp.float32) + arrived[k, s, o].astype(jnp.float32)
                ).astype(jnp.bfloat16)
            if t + 1 < bits:
                for s in sent_in(o, t + 1):
                    part_copy(k, s, o, order(o)[t + 1]).start()

    def row_at(k):
        return (my_row + 1 + k) % row_count

    def cross_copy(k):
        return pltpu.make_async_remote_copy(
            packed.at[k, 0], crossed.at[k], cross_send.at[k], cross_recv.at[k],
            device_id={"band": row_at(k) * group + mine},
        )

    for k in range(row_count):
        r = row_at(k)

        for i in range(group):
            s = group - 1 - i
            owner = 0
            for b in range(bits):
                owner = owner + ((s // (1 << b) + mine // (1 << b)) % 2) * (1 << b)
            for o in range(pairs):
                c = owner * owned + 2 * o
                both = pack_pair(*density_pair(r, c))
                packed[k, s, o] = both.astype(jnp.bfloat16)
            for o in range(pairs):
                if s in sent_in(o, 0):
                    part_copy(k, s, o, order(o)[0]).start()
            if k > 0 and i == group // 2 - 1:
                fold(k - 1, 0)
        if k > 0:
            for t in range(1, bits):
                fold(k - 1, t)
            cross_copy(k - 1).start()

    for t in range(bits):
        fold(last, t)
    for k in range(last):
        cross_copy(k).wait_recv()
    for o in range(pairs):
        total = packed[last, 0, o].astype(jnp.float32)
        for k in range(last):
            total = total + crossed[k, o].astype(jnp.float32)
        first, second = unpack_pair(total / total_bands)
        out_ref[2 * o] = first
        out_ref[2 * o + 1] = second

    for up, down in halos:
        up.wait_send()
        down.wait_send()
    for k in range(row_count):
        for o in range(pairs):
            for t in range(bits):
                for s in sent_in(o, t):
                    part_copy(k, s, o, order(o)[t]).wait_send()
        if k < last:
            cross_copy(k).wait_send()


def local(strips, bands, coeffs, hamiltonian, adjacency, occupation):
    elems, basis, columns = coeffs.shape
    row_count = elems // EY
    group = bands // row_count
    owned = EY // group
    assert group * row_count == bands and group * owned == EY and group & (group - 1) == 0
    assert owned % 2 == 0 and row_count >= 3 and strips >= 2 and columns == basis
    edge = pltpu.VMEM((EY, basis, columns), jnp.bfloat16)
    own = pltpu.VMEM((elems, basis, columns), jnp.bfloat16)
    field = pltpu.VMEM((elems + 2 * EY, basis, columns), jnp.bfloat16)
    block = (owned // 2, basis + PAD, basis)
    wide = -(-elems // 128) * 128
    dma = pltpu.SemaphoreType.DMA
    flops = 2 * elems * basis * basis * columns * 16
    return pl.pallas_call(
        functools.partial(kernel, strips, bands, float(columns * bands)),
        out_shape=jax.ShapeDtypeStruct((owned, basis, basis), jnp.float32),
        in_specs=[
            pl.BlockSpec(memory_space=pl.ANY),
            pl.BlockSpec(memory_space=pl.ANY),
            pl.BlockSpec(memory_space=pl.ANY),
            pl.BlockSpec(memory_space=pl.ANY),
        ],
        out_specs=pl.BlockSpec(memory_space=pltpu.VMEM),
        scratch_shapes=[
            pltpu.VMEM((elems * 5, basis, basis), jnp.bfloat16),
            own, edge, edge, field, field,
            pltpu.VMEM((row_count, group) + block, jnp.bfloat16),
            pltpu.VMEM((row_count, group) + block, jnp.bfloat16),
            pltpu.VMEM((row_count - 1,) + block, jnp.bfloat16),
            pltpu.VMEM((5, elems), jnp.int32),
            pltpu.VMEM((1, columns), jnp.float32),
            pltpu.VMEM((16, wide), jnp.int32),
            pltpu.SMEM((16, wide), jnp.int32),
            dma((row_count,)), dma((4,)), dma((6,)), dma((6,)),
            dma((row_count, group, owned // 2)), dma((row_count, group, owned // 2)),
            dma((row_count - 1,)), dma((row_count - 1,)),
        ],
        compiler_params=pltpu.CompilerParams(
            collective_id=0, has_side_effects=True, vmem_limit_bytes=62 * MIB
        ),
        cost_estimate=pl.CostEstimate(
            flops=flops, bytes_accessed=2 * elems * basis * (5 * basis + columns), transcendentals=0
        ),
        name="chebyshev_density",
    )(
        adjacency.T,
        occupation.reshape(1, columns),
        coeffs,
        hamiltonian.reshape(elems * 5, basis, basis),
    )


def solution(mesh):
    return jax.shard_map(
        functools.partial(local, mesh.shape["strip"], mesh.shape["band"]),
        mesh=mesh,
        in_specs=(
            P("strip", None, "band"),
            P("strip", None, None, None),
            P("strip", None),
            P("band"),
        ),
        out_specs=P(("strip", "band"), None, None),
        check_vma=False,
    )
```

```python
import functools
import jax
import jax.numpy as jnp
from jax import lax
from jax.experimental import pallas as pl
from jax.experimental.pallas import tpu as pltpu
from jax.sharding import PartitionSpec as P

EY = 16
PAD = 16
MIB = 1 << 20


def lanes(shape):
    return lax.broadcasted_iota(jnp.int32, shape, 1)


def rows(shape):
    return lax.broadcasted_iota(jnp.int32, shape, 0)


def pack_pair(first, second):
    half = first.shape[0] // 2
    left = lanes((half, 2 * half)) < half
    lane = jnp.where(left, lanes(left.shape), lanes(left.shape) - half)
    row = rows(left.shape)
    blocks_1 = jnp.where(left, first[:half], first[half:])
    blocks_2 = jnp.where(left, second[:half], second[half:])
    triangles = jnp.where(row >= lane, blocks_1, blocks_2)
    corners = jnp.where(left, second[half:], first[:half])
    diagonal = jnp.sum(jnp.where(row == lane, blocks_2, 0.0), axis=0, keepdims=True)
    return jnp.concatenate(
        [triangles, corners, jnp.broadcast_to(diagonal, (PAD, 2 * half))], axis=0
    )


def unpack_pair(packed):
    nb = packed.shape[1]
    half = nb // 2
    triangles, corners, diagonal = packed[:half], packed[half:nb], packed[nb:nb + 1]
    left = lanes((half, nb)) < half
    i, j = rows((nb, nb)), lanes((nb, nb))
    same = (i < half) == (j < half)
    wide_1 = jnp.concatenate([jnp.where(left, triangles, corners), triangles], axis=0)
    held_1 = (same & (i >= j)) | ((i < half) & (j >= half))
    first = jnp.where(held_1, wide_1, wide_1.T)
    wide_2 = jnp.concatenate([triangles, jnp.where(left, corners, triangles)], axis=0)
    held_2 = (same & (i < j)) | ((i >= half) & (j < half))
    second = jnp.where(held_2, wide_2, wide_2.T)
    second = jnp.where(i == j, jnp.broadcast_to(diagonal, (nb, nb)), second)
    return first, second


def kernel(
    strips, bands, total_bands,
    adj_hbm, occ_hbm, coeffs_hbm, ham_hbm, out_ref,
    ham, v0, v0_first, v0_last, v1, v2, packed, arrived, crossed, adj_ref, occ_ref, table, slots,
    ham_sem, own_sem, halo_send, halo_recv, part_send, part_recv, cross_send, cross_recv,
):
    elems = coeffs_hbm.shape[0]
    row_count = elems // EY
    group = bands // row_count
    bits = group.bit_length() - 1
    owned = EY // group
    pairs = owned // 2
    strip = lax.axis_index("strip")
    band = lax.axis_index("band")
    my_row, mine = band // group, band % group
    above, below = (strip + strips - 1) % strips, (strip + 1) % strips

    def partner(bit):
        step = 1 << bit
        return band + step * (1 - 2 * ((band // step) % 2))

    adj_copy = pltpu.make_async_copy(adj_hbm, adj_ref, own_sem.at[0])
    occ_copy = pltpu.make_async_copy(occ_hbm, occ_ref, own_sem.at[1])
    own_copy = pltpu.make_async_copy(coeffs_hbm, v0, own_sem.at[2])
    table_copy = pltpu.make_async_copy(table, slots, own_sem.at[3])
    adj_copy.start()
    own_copy.start()
    per_row = EY * 5
    ham_copies = [
        pltpu.make_async_copy(
            ham_hbm.at[pl.ds(r * per_row, per_row)], ham.at[pl.ds(r * per_row, per_row)], ham_sem.at[r]
        )
        for r in range(row_count)
    ]
    last = row_count - 1
    first_order = list(range(1, last)) + [0, last]
    row_order = [1, 0, last] + list(range(2, last))
    for r in first_order:
        ham_copies[r].start()
    occ_copy.start()

    barrier = pltpu.get_barrier_semaphore()
    greeted = 0
    for target in [above] if strips == 2 else [above, below]:
        pl.semaphore_signal(barrier, inc=1, device_id={"strip": target})
        greeted += 1
    for bit in range(bits):
        pl.semaphore_signal(barrier, inc=1, device_id={"band": partner(bit)})
        greeted += 1
    for away in range(1, row_count):
        pl.semaphore_signal(
            barrier, inc=1, device_id={"band": ((my_row + away) % row_count) * group + mine}
        )
        greeted += 1

    adj_copy.wait()
    sheet_rows = row_count * strips
    a = adj_ref[...]
    places = lax.rem(lax.div(a, EY) - strip * row_count + sheet_rows, sheet_rows) * EY + lax.rem(a, EY)
    here = lanes((1, elems))
    line, col = lax.div(here, EY), lax.rem(here, EY)
    wanted = [
        here,
        lax.rem(line + sheet_rows - 1, sheet_rows) * EY + col,
        lax.rem(line + 1, sheet_rows) * EY + col,
        line * EY + lax.rem(col + EY - 1, EY),
        line * EY + lax.rem(col + 1, EY),
    ]
    for d in range(5):
        slot = here * 0
        for j in range(1, 5):
            slot = slot + jnp.where(places[j:j + 1] == wanted[d], j, 0)
        table[d:d + 1, :elems] = jnp.minimum(slot, 4)
        table[8 + d:9 + d, :elems] = jnp.minimum(places[d:d + 1], elems - 1)
    table_copy.start()
    pl.semaphore_wait(barrier, greeted)

    def halo(field, source, shift, first, final):
        up = pltpu.make_async_remote_copy(
            source.at[pl.ds(shift, EY)], final,
            halo_send.at[2 * field], halo_recv.at[2 * field], device_id={"strip": above},
        )
        down = pltpu.make_async_remote_copy(
            source.at[pl.ds(shift + elems - EY, EY)], first,
            halo_send.at[2 * field + 1], halo_recv.at[2 * field + 1], device_id={"strip": below},
        )
        return up, down

    ends = [(v.at[pl.ds(0, EY)], v.at[pl.ds(EY + elems, EY)]) for v in (v1, v2)]
    halos = [
        halo(0, coeffs_hbm, 0, v0_first, v0_last), halo(1, v1, EY, *ends[0]), halo(2, v2, EY, *ends[1])
    ]
    for copy in halos[0]:
        copy.start()

    def product(blocks, fields):
        return jnp.dot(
            jnp.concatenate(blocks, axis=1), jnp.concatenate(fields, axis=0),
            preferred_element_type=jnp.float32,
        )

    def inner_element(r, c):
        e = r * EY + c
        out = product(
            [ham[e * 5 + j] for j in range(5)], [v0[slots[8 + j, e]] for j in range(5)]
        )
        v1[e + EY] = out.astype(jnp.bfloat16)

    def blocks_of(e):
        return [ham[e * 5 + slots[d, e]] for d in range(5)]

    def pair_product(e, field, above_of, below_of, line, c):
        first, second = blocks_of(e), blocks_of(e + 1)
        between = product(
            [
                jnp.concatenate([first[0], second[3]], axis=0),
                jnp.concatenate([first[4], second[0]], axis=0),
            ],
            [field[line + c], field[line + c + 1]],
        )
        rest_1 = product(
            first[1:4], [above_of(c), below_of(c), field[line + lax.rem(c + EY - 1, EY)]]
        )
        rest_2 = product(
            [second[1], second[2], second[4]],
            [above_of(c + 1), below_of(c + 1), field[line + lax.rem(c + 2, EY)]],
        )
        return between[:rest_1.shape[0]] + rest_1, between[rest_1.shape[0]:] + rest_2

    def outer_pair(r, c):
        line = r * EY
        pair = pair_product(
            line + c, v0,
            lambda at: v0_first[at] if r == 0 else v0[line - EY + at],
            lambda at: v0_last[at] if r == last else v0[line + EY + at],
            line, c,
        )
        for m in range(2):
            v1[line + c + m + EY] = pair[m].astype(jnp.bfloat16)

    def later_pair(ref, r, c):
        line = (r + 1) * EY
        return pair_product(
            r * EY + c, ref, lambda at: ref[line - EY + at], lambda at: ref[line + EY + at], line, c
        )

    def second_pair(r, c):
        e = r * EY + c
        pair = later_pair(v1, r, c)
        for m in range(2):
            out = 2.0 * pair[m] - v0[e + m].astype(jnp.float32)
            v2[e + m + EY] = out.astype(jnp.bfloat16)

    def one_row(step, element, r):
        for c in range(0, EY, step):
            element(r, c)

    own_copy.wait()
    table_copy.wait()
    for r in first_order[:-2]:
        ham_copies[r].wait()
        one_row(1, inner_element, r)
    for r in (0, last):
        ham_copies[r].wait()
    for copy in halos[0]:
        copy.wait_recv()
    for r in (0, last):
        one_row(2, outer_pair, r)
        if r == 0:
            halos[1][0].start()
        if r == row_count - 1:
            halos[1][1].start()
    for r in row_order:
        if r == 0:
            halos[1][1].wait_recv()
        if r == row_count - 1:
            halos[1][0].wait_recv()
        one_row(2, second_pair, r)
        if r == 0:
            halos[2][0].start()
        if r == row_count - 1:
            halos[2][1].start()
    for copy in halos[2]:
        copy.wait_recv()

    occ_copy.wait()
    occ = occ_ref[...]

    def density_pair(r, c):
        parts = []
        for m, product_m in enumerate(later_pair(v2, r, c)):
            out = 2.0 * product_m - v1[r * EY + c + m + EY].astype(jnp.float32)
            filtered = out.astype(jnp.bfloat16)
            weighted = (filtered.astype(jnp.float32) * occ).astype(jnp.bfloat16)
            parts.append(lax.dot_general(
                weighted, filtered, (((1,), (1,)), ((), ())), preferred_element_type=jnp.float32
            ))
        return parts

    def order(o):
        return [(o + t) % bits for t in range(bits)]

    def part_copy(k, s, o, bit):
        return pltpu.make_async_remote_copy(
            packed.at[k, s, o], arrived.at[k, s, o],
            part_send.at[k, s, o], part_recv.at[k, s, o], device_id={"band": partner(bit)},
        )

    def sent_in(o, t):
        seq = order(o)
        return [
            s for s in range(group)
            if s >> seq[t] & 1 and not any(s >> b & 1 for b in seq[:t])
        ]

    def fold(k, t, passed_on=True, own=True):
        for keep_own in [False] * passed_on + [True] * own:
            for o in range(pairs):
                bit = order(o)[t]
                for s in sent_in(o, t):
                    kept = s - (1 << bit)
                    if (kept == 0) != keep_own:
                        continue
                    part_copy(k, s, o, bit).wait_recv()
                    packed[k, kept, o] = (
                        packed[k, kept, o].astype(jnp.float32) + arrived[k, s, o].astype(jnp.float32)
                    ).astype(jnp.bfloat16)
                if t + 1 < bits and not keep_own:
                    for s in sent_in(o, t + 1):
                        part_copy(k, s, o, order(o)[t + 1]).start()

    def row_at(k):
        return (my_row + 1 + k) % row_count

    def cross_copy(k):
        return pltpu.make_async_remote_copy(
            packed.at[k, 0], crossed.at[k], cross_send.at[k], cross_recv.at[k],
            device_id={"band": row_at(k) * group + mine},
        )

    for k in range(row_count):
        r = row_at(k)

        for i in range(group):
            s = group - 1 - i
            owner = 0
            for b in range(bits):
                owner = owner + ((s // (1 << b) + mine // (1 << b)) % 2) * (1 << b)
            for o in range(pairs):
                c = owner * owned + 2 * o
                both = pack_pair(*density_pair(r, c))
                packed[k, s, o] = both.astype(jnp.bfloat16)
            for o in range(pairs):
                if s in sent_in(o, 0):
                    part_copy(k, s, o, order(o)[0]).start()
            if k > 0 and i == group // 2 - 1:
                fold(k - 1, 0)
            if k > 0 and i == group - 2:
                for t in range(1, bits):
                    fold(k - 1, t)
                cross_copy(k - 1).start()
                if k == last:
                    fold(last, 0, own=False)

    fold(last, 0, passed_on=False)
    for t in range(1, bits):
        fold(last, t)
    for k in range(last):
        cross_copy(k).wait_recv()
    for o in range(pairs):
        total = packed[last, 0, o].astype(jnp.float32)
        for k in range(last):
            total = total + crossed[k, o].astype(jnp.float32)
        first, second = unpack_pair(total / total_bands)
        out_ref[2 * o] = first
        out_ref[2 * o + 1] = second

    for up, down in halos:
        up.wait_send()
        down.wait_send()
    for k in range(row_count):
        for o in range(pairs):
            for t in range(bits):
                for s in sent_in(o, t):
                    part_copy(k, s, o, order(o)[t]).wait_send()
        if k < last:
            cross_copy(k).wait_send()


def local(strips, bands, coeffs, hamiltonian, adjacency, occupation):
    elems, basis, columns = coeffs.shape
    row_count = elems // EY
    group = bands // row_count
    owned = EY // group
    assert group * row_count == bands and group * owned == EY and group & (group - 1) == 0
    assert owned % 2 == 0 and row_count >= 3 and strips >= 2 and columns == basis
    edge = pltpu.VMEM((EY, basis, columns), jnp.bfloat16)
    own = pltpu.VMEM((elems, basis, columns), jnp.bfloat16)
    field = pltpu.VMEM((elems + 2 * EY, basis, columns), jnp.bfloat16)
    block = (owned // 2, basis + PAD, basis)
    wide = -(-elems // 128) * 128
    dma = pltpu.SemaphoreType.DMA
    flops = 2 * elems * basis * basis * columns * 16
    return pl.pallas_call(
        functools.partial(kernel, strips, bands, float(columns * bands)),
        out_shape=jax.ShapeDtypeStruct((owned, basis, basis), jnp.float32),
        in_specs=[
            pl.BlockSpec(memory_space=pl.ANY),
            pl.BlockSpec(memory_space=pl.ANY),
            pl.BlockSpec(memory_space=pl.ANY),
            pl.BlockSpec(memory_space=pl.ANY),
        ],
        out_specs=pl.BlockSpec(memory_space=pltpu.VMEM),
        scratch_shapes=[
            pltpu.VMEM((elems * 5, basis, basis), jnp.bfloat16),
            own, edge, edge, field, field,
            pltpu.VMEM((row_count, group) + block, jnp.bfloat16),
            pltpu.VMEM((row_count, group) + block, jnp.bfloat16),
            pltpu.VMEM((row_count - 1,) + block, jnp.bfloat16),
            pltpu.VMEM((5, elems), jnp.int32),
            pltpu.VMEM((1, columns), jnp.float32),
            pltpu.VMEM((16, wide), jnp.int32),
            pltpu.SMEM((16, wide), jnp.int32),
            dma((row_count,)), dma((4,)), dma((6,)), dma((6,)),
            dma((row_count, group, owned // 2)), dma((row_count, group, owned // 2)),
            dma((row_count - 1,)), dma((row_count - 1,)),
        ],
        compiler_params=pltpu.CompilerParams(
            collective_id=0, has_side_effects=True, vmem_limit_bytes=62 * MIB
        ),
        cost_estimate=pl.CostEstimate(
            flops=flops, bytes_accessed=2 * elems * basis * (5 * basis + columns), transcendentals=0
        ),
        name="chebyshev_density",
    )(
        adjacency.T,
        occupation.reshape(1, columns),
        coeffs,
        hamiltonian.reshape(elems * 5, basis, basis),
    )


def solution(mesh):
    return jax.shard_map(
        functools.partial(local, mesh.shape["strip"], mesh.shape["band"]),
        mesh=mesh,
        in_specs=(
            P("strip", None, "band"),
            P("strip", None, None, None),
            P("strip", None),
            P("band"),
        ),
        out_specs=P(("strip", "band"), None, None),
        check_vma=False,
    )
```

```python
import functools
import jax
import jax.numpy as jnp
from jax import lax
from jax.experimental import pallas as pl
from jax.experimental.pallas import tpu as pltpu
from jax.sharding import PartitionSpec as P

EY = 16
PAD = 16
MIB = 1 << 20


def lanes(shape):
    return lax.broadcasted_iota(jnp.int32, shape, 1)


def rows(shape):
    return lax.broadcasted_iota(jnp.int32, shape, 0)


def pack_pair(first, second):
    half = first.shape[0] // 2
    left = lanes((half, 2 * half)) < half
    lane = jnp.where(left, lanes(left.shape), lanes(left.shape) - half)
    row = rows(left.shape)
    blocks_1 = jnp.where(left, first[:half], first[half:])
    blocks_2 = jnp.where(left, second[:half], second[half:])
    triangles = jnp.where(row >= lane, blocks_1, blocks_2)
    corners = jnp.where(left, second[half:], first[:half])
    diagonal = jnp.sum(jnp.where(row == lane, blocks_2, 0.0), axis=0, keepdims=True)
    return jnp.concatenate(
        [triangles, corners, jnp.broadcast_to(diagonal, (PAD, 2 * half))], axis=0
    )


def unpack_pair(packed):
    nb = packed.shape[1]
    half = nb // 2
    triangles, corners, diagonal = packed[:half], packed[half:nb], packed[nb:nb + 1]
    left = lanes((half, nb)) < half
    i, j = rows((nb, nb)), lanes((nb, nb))
    same = (i < half) == (j < half)
    wide_1 = jnp.concatenate([jnp.where(left, triangles, corners), triangles], axis=0)
    held_1 = (same & (i >= j)) | ((i < half) & (j >= half))
    first = jnp.where(held_1, wide_1, wide_1.T)
    wide_2 = jnp.concatenate([triangles, jnp.where(left, corners, triangles)], axis=0)
    held_2 = (same & (i < j)) | ((i >= half) & (j < half))
    second = jnp.where(held_2, wide_2, wide_2.T)
    second = jnp.where(i == j, jnp.broadcast_to(diagonal, (nb, nb)), second)
    return first, second


def kernel(
    strips, bands, total_bands,
    adj_hbm, occ_hbm, coeffs_hbm, ham_hbm, out_ref,
    ham, v0, v0_first, v0_last, v1, v2, packed, arrived, crossed, adj_ref, occ_ref, table, slots,
    ham_sem, own_sem, halo_send, halo_recv, part_send, part_recv, cross_send, cross_recv,
):
    elems = coeffs_hbm.shape[0]
    row_count = elems // EY
    group = bands // row_count
    bits = group.bit_length() - 1
    owned = EY // group
    pairs = owned // 2
    strip = lax.axis_index("strip")
    band = lax.axis_index("band")
    my_row, mine = band // group, band % group
    above, below = (strip + strips - 1) % strips, (strip + 1) % strips

    def partner(bit):
        step = 1 << bit
        return band + step * (1 - 2 * ((band // step) % 2))

    adj_copy = pltpu.make_async_copy(adj_hbm, adj_ref, own_sem.at[0])
    occ_copy = pltpu.make_async_copy(occ_hbm, occ_ref, own_sem.at[1])
    own_copy = pltpu.make_async_copy(coeffs_hbm, v0, own_sem.at[2])
    table_copy = pltpu.make_async_copy(table, slots, own_sem.at[3])
    adj_copy.start()
    own_copy.start()
    per_row = EY * 5
    ham_copies = [
        pltpu.make_async_copy(
            ham_hbm.at[pl.ds(r * per_row, per_row)], ham.at[pl.ds(r * per_row, per_row)], ham_sem.at[r]
        )
        for r in range(row_count)
    ]
    last = row_count - 1
    first_order = list(range(1, last)) + [0, last]
    row_order = [1, 0, last] + list(range(2, last))
    for r in first_order:
        ham_copies[r].start()
    occ_copy.start()

    barrier = pltpu.get_barrier_semaphore()
    greeted = 0
    for target in [above] if strips == 2 else [above, below]:
        pl.semaphore_signal(barrier, inc=1, device_id={"strip": target})
        greeted += 1
    for bit in range(bits):
        pl.semaphore_signal(barrier, inc=1, device_id={"band": partner(bit)})
        greeted += 1
    for away in range(1, row_count):
        pl.semaphore_signal(
            barrier, inc=1, device_id={"band": ((my_row + away) % row_count) * group + mine}
        )
        greeted += 1

    adj_copy.wait()
    sheet_rows = row_count * strips
    a = adj_ref[...]
    places = lax.rem(lax.div(a, EY) - strip * row_count + sheet_rows, sheet_rows) * EY + lax.rem(a, EY)
    here = lanes((1, elems))
    line, col = lax.div(here, EY), lax.rem(here, EY)
    wanted = [
        here,
        lax.rem(line + sheet_rows - 1, sheet_rows) * EY + col,
        lax.rem(line + 1, sheet_rows) * EY + col,
        line * EY + lax.rem(col + EY - 1, EY),
        line * EY + lax.rem(col + 1, EY),
    ]
    for d in range(5):
        slot = here * 0
        for j in range(1, 5):
            slot = slot + jnp.where(places[j:j + 1] == wanted[d], j, 0)
        table[d:d + 1, :elems] = jnp.minimum(slot, 4)
        table[8 + d:9 + d, :elems] = jnp.minimum(places[d:d + 1], elems - 1)
    table_copy.start()
    pl.semaphore_wait(barrier, greeted)

    def halo(field, source, shift, first, final):
        up = pltpu.make_async_remote_copy(
            source.at[pl.ds(shift, EY)], final,
            halo_send.at[2 * field], halo_recv.at[2 * field], device_id={"strip": above},
        )
        down = pltpu.make_async_remote_copy(
            source.at[pl.ds(shift + elems - EY, EY)], first,
            halo_send.at[2 * field + 1], halo_recv.at[2 * field + 1], device_id={"strip": below},
        )
        return up, down

    ends = [(v.at[pl.ds(0, EY)], v.at[pl.ds(EY + elems, EY)]) for v in (v1, v2)]
    halos = [
        halo(0, coeffs_hbm, 0, v0_first, v0_last), halo(1, v1, EY, *ends[0]), halo(2, v2, EY, *ends[1])
    ]
    for copy in halos[0]:
        copy.start()

    def product(blocks, fields):
        return jnp.dot(
            jnp.concatenate(blocks, axis=1), jnp.concatenate(fields, axis=0),
            preferred_element_type=jnp.float32,
        )

    def inner_element(r, c):
        e = r * EY + c
        out = product(
            [ham[e * 5 + j] for j in range(5)], [v0[slots[8 + j, e]] for j in range(5)]
        )
        v1[e + EY] = out.astype(jnp.bfloat16)

    def blocks_of(e):
        return [ham[e * 5 + slots[d, e]] for d in range(5)]

    def pair_product(e, field, above_of, below_of, line, c):
        first, second = blocks_of(e), blocks_of(e + 1)
        between = product(
            [
                jnp.concatenate([first[0], second[3]], axis=0),
                jnp.concatenate([first[4], second[0]], axis=0),
            ],
            [field[line + c], field[line + c + 1]],
        )
        rest_1 = product(
            first[1:4], [above_of(c), below_of(c), field[line + lax.rem(c + EY - 1, EY)]]
        )
        rest_2 = product(
            [second[1], second[2], second[4]],
            [above_of(c + 1), below_of(c + 1), field[line + lax.rem(c + 2, EY)]],
        )
        return between[:rest_1.shape[0]] + rest_1, between[rest_1.shape[0]:] + rest_2

    def outer_pair(r, c):
        line = r * EY
        pair = pair_product(
            line + c, v0,
            lambda at: v0_first[at] if r == 0 else v0[line - EY + at],
            lambda at: v0_last[at] if r == last else v0[line + EY + at],
            line, c,
        )
        for m in range(2):
            v1[line + c + m + EY] = pair[m].astype(jnp.bfloat16)

    def later_pair(ref, r, c):
        line = (r + 1) * EY
        return pair_product(
            r * EY + c, ref, lambda at: ref[line - EY + at], lambda at: ref[line + EY + at], line, c
        )

    def second_pair(r, c):
        e = r * EY + c
        pair = later_pair(v1, r, c)
        for m in range(2):
            out = 2.0 * pair[m] - v0[e + m].astype(jnp.float32)
            v2[e + m + EY] = out.astype(jnp.bfloat16)

    def one_row(step, element, r):
        for c in range(0, EY, step):
            element(r, c)

    own_copy.wait()
    table_copy.wait()
    for r in first_order[:-2]:
        ham_copies[r].wait()
        one_row(1, inner_element, r)
    for r in (0, last):
        ham_copies[r].wait()
    for copy in halos[0]:
        copy.wait_recv()
    for r in (0, last):
        one_row(2, outer_pair, r)
        if r == 0:
            halos[1][0].start()
        if r == row_count - 1:
            halos[1][1].start()
    for r in row_order:
        if r == 0:
            halos[1][1].wait_recv()
        if r == row_count - 1:
            halos[1][0].wait_recv()
        one_row(2, second_pair, r)
        if r == 0:
            halos[2][0].start()
        if r == row_count - 1:
            halos[2][1].start()
    for copy in halos[2]:
        copy.wait_recv()

    occ_copy.wait()
    occ = occ_ref[...]

    def density_pair(r, c):
        parts = []
        for m, product_m in enumerate(later_pair(v2, r, c)):
            out = 2.0 * product_m - v1[r * EY + c + m + EY].astype(jnp.float32)
            filtered = out.astype(jnp.bfloat16)
            weighted = (filtered.astype(jnp.float32) * occ).astype(jnp.bfloat16)
            parts.append(lax.dot_general(
                weighted, filtered, (((1,), (1,)), ((), ())), preferred_element_type=jnp.float32
            ))
        return parts

    def order(o):
        return [(o + t) % bits for t in range(bits)]

    def part_copy(k, s, o, bit):
        return pltpu.make_async_remote_copy(
            packed.at[k, s, o], arrived.at[k, s, o],
            part_send.at[k, s, o], part_recv.at[k, s, o], device_id={"band": partner(bit)},
        )

    def sent_in(o, t):
        seq = order(o)
        return [
            s for s in range(group)
            if s >> seq[t] & 1 and not any(s >> b & 1 for b in seq[:t])
        ]

    def fold(k, t):
        for o in range(pairs):
            bit = order(o)[t]
            for s in sent_in(o, t):
                part_copy(k, s, o, bit).wait_recv()
                kept = s - (1 << bit)
                packed[k, kept, o] = (
                    packed[k, kept, o].astype(jnp.float32) + arrived[k, s, o].astype(jnp.float32)
                ).astype(jnp.bfloat16)
            if t + 1 < bits:
                for s in sent_in(o, t + 1):
                    part_copy(k, s, o, order(o)[t + 1]).start()

    def row_at(k):
        return (my_row + 1 + k) % row_count

    def cross_copy(k):
        return pltpu.make_async_remote_copy(
            packed.at[k, 0], crossed.at[k], cross_send.at[k], cross_recv.at[k],
            device_id={"band": row_at(k) * group + mine},
        )

    def pass_on(k):
        for t in range(1, bits):
            fold(k, t)
        cross_copy(k).start()

    for k in range(row_count):
        r = row_at(k)

        for i in range(group):
            s = group - 1 - i
            owner = 0
            for b in range(bits):
                owner = owner + ((s // (1 << b) + mine // (1 << b)) % 2) * (1 << b)
            for o in range(pairs):
                c = owner * owned + 2 * o
                both = pack_pair(*density_pair(r, c))
                packed[k, s, o] = both.astype(jnp.bfloat16)
            for o in range(pairs):
                if s in sent_in(o, 0):
                    part_copy(k, s, o, order(o)[0]).start()
            if k > 1 and i == group // 2 - 1:
                pass_on(k - 2)
        if k > 0:
            fold(k - 1, 0)

    pass_on(last - 1)
    for t in range(bits):
        fold(last, t)
    for k in range(last):
        cross_copy(k).wait_recv()
    for o in range(pairs):
        total = packed[last, 0, o].astype(jnp.float32)
        for k in range(last):
            total = total + crossed[k, o].astype(jnp.float32)
        first, second = unpack_pair(total / total_bands)
        out_ref[2 * o] = first
        out_ref[2 * o + 1] = second

    for up, down in halos:
        up.wait_send()
        down.wait_send()
    for k in range(row_count):
        for o in range(pairs):
            for t in range(bits):
                for s in sent_in(o, t):
                    part_copy(k, s, o, order(o)[t]).wait_send()
        if k < last:
            cross_copy(k).wait_send()


def local(strips, bands, coeffs, hamiltonian, adjacency, occupation):
    elems, basis, columns = coeffs.shape
    row_count = elems // EY
    group = bands // row_count
    owned = EY // group
    assert group * row_count == bands and group * owned == EY and group & (group - 1) == 0
    assert owned % 2 == 0 and row_count >= 3 and strips >= 2 and columns == basis
    edge = pltpu.VMEM((EY, basis, columns), jnp.bfloat16)
    own = pltpu.VMEM((elems, basis, columns), jnp.bfloat16)
    field = pltpu.VMEM((elems + 2 * EY, basis, columns), jnp.bfloat16)
    block = (owned // 2, basis + PAD, basis)
    wide = -(-elems // 128) * 128
    dma = pltpu.SemaphoreType.DMA
    flops = 2 * elems * basis * basis * columns * 16
    return pl.pallas_call(
        functools.partial(kernel, strips, bands, float(columns * bands)),
        out_shape=jax.ShapeDtypeStruct((owned, basis, basis), jnp.float32),
        in_specs=[
            pl.BlockSpec(memory_space=pl.ANY),
            pl.BlockSpec(memory_space=pl.ANY),
            pl.BlockSpec(memory_space=pl.ANY),
            pl.BlockSpec(memory_space=pl.ANY),
        ],
        out_specs=pl.BlockSpec(memory_space=pltpu.VMEM),
        scratch_shapes=[
            pltpu.VMEM((elems * 5, basis, basis), jnp.bfloat16),
            own, edge, edge, field, field,
            pltpu.VMEM((row_count, group) + block, jnp.bfloat16),
            pltpu.VMEM((row_count, group) + block, jnp.bfloat16),
            pltpu.VMEM((row_count - 1,) + block, jnp.bfloat16),
            pltpu.VMEM((5, elems), jnp.int32),
            pltpu.VMEM((1, columns), jnp.float32),
            pltpu.VMEM((16, wide), jnp.int32),
            pltpu.SMEM((16, wide), jnp.int32),
            dma((row_count,)), dma((4,)), dma((6,)), dma((6,)),
            dma((row_count, group, owned // 2)), dma((row_count, group, owned // 2)),
            dma((row_count - 1,)), dma((row_count - 1,)),
        ],
        compiler_params=pltpu.CompilerParams(
            collective_id=0, has_side_effects=True, vmem_limit_bytes=62 * MIB
        ),
        cost_estimate=pl.CostEstimate(
            flops=flops, bytes_accessed=2 * elems * basis * (5 * basis + columns), transcendentals=0
        ),
        name="chebyshev_density",
    )(
        adjacency.T,
        occupation.reshape(1, columns),
        coeffs,
        hamiltonian.reshape(elems * 5, basis, basis),
    )


def solution(mesh):
    return jax.shard_map(
        functools.partial(local, mesh.shape["strip"], mesh.shape["band"]),
        mesh=mesh,
        in_specs=(
            P("strip", None, "band"),
            P("strip", None, None, None),
            P("strip", None),
            P("band"),
        ),
        out_specs=P(("strip", "band"), None, None),
        check_vma=False,
    )
```
